512 devices in a mesh: seq: 8 (over y, core), dp: 64 (over z, x).
Axes of the slice: x: 4, y: 4, z: 16, core: 2. Of those that a mesh axis runs over, the one named last changes fastest.
Arguments:
- frames: bfloat16 [128, 512, 1024], P('dp', 'seq'), may hold values from -6 to 6
- lengths: int32 [128], P('dp'), may hold values from 128 to 512, as said below
- w_qkv: bfloat16 [1024, 3072], P('dp'), may hold values from -4 to 4
- w_out: bfloat16 [1024, 1024], P('dp'), may hold values from -0.1875 to 0.1875
- w_point: bfloat16 [1024, 1024], P('dp'), may hold values from -0.1875 to 0.1875
- w_depth: float32 [9, 1024], replicated, may hold values from -2 to 2
Outputs:
- layer_out: bfloat16 [128, 512, 1024], P('dp', 'seq')
The draws below stay inside these ranges and needn't reach their ends.
Inputs may be any that keep to these rules, and one draw needn't show every extreme that they name: `lengths`: every recording has at least 128 valid frames; some recording fills all 512.
All inputs are finite; a program needn't handle non-finite values.
Results may differ from the reference program's by a relative error of at most 0.014.
Values may be sent and summed in bfloat16 or wider, within the bound.
A program may use at most 64 MiB of HBM per device.

```python
import jax
import jax.numpy as jnp
from jax import lax

D = 1024
HEADS = 8
KERNEL = 9
HDIM = 128
LEN = 512
UTTS = 128


def draw_lengths(key, part):
    first = jax.random.fold_in(key, 11)
    second = jax.random.fold_in(key, 12)
    drawn = jax.random.randint(first, (UTTS,), LEN // 4, LEN + 1)
    order = jax.random.permutation(second, UTTS)
    drawn = drawn.at[order[0]].set(LEN)
    drawn = drawn.at[order[1]].set(LEN // 4)
    return drawn.astype(jnp.int32)


def draw_w_qkv(key, part):
    first = jax.random.fold_in(key, 21)
    base = jax.random.normal(first, (D, 3 * D), jnp.float32) * D ** (-0.5)
    column = jnp.arange(3 * D)
    scaling = jnp.where(column < D, 2.5, 1.0)
    result = base * scaling[None, :]
    return jnp.clip(result, -4.0, 4.0).astype(jnp.bfloat16)


def block_levels(stream_key, extent, shards, least, top_value):
    factor_of, own = 1.0, jax.random.fold_in(stream_key, 6)
    for axis_at, parts in shards:
        draws = jnp.exp(jax.random.uniform(jax.random.fold_in(own, axis_at), (parts,), jnp.float32, least / len(shards), top_value / len(shards)))
        factor_of = factor_of * jnp.repeat(draws, extent[axis_at] // parts).reshape([-1 if axis == axis_at else 1 for axis in range(len(extent))])
    return factor_of


def normal_values(stream_key, dims, deviation, limit, cuts=(), dtype=jnp.bfloat16):
    array = deviation * jax.random.normal(stream_key, dims, jnp.float32)
    if cuts:
        array = array * block_levels(stream_key, dims, cuts, -0.22, 0.18)
    return jnp.clip(array, -limit, limit).astype(dtype)


def setup_inputs(seed: int = 0) -> dict:
    splits = jax.random.split(jax.random.key(seed), 7)
    return {
        "frames": normal_values(splits[0], (UTTS, LEN, D), 1.0, 6.0, ((0, 64), (1, 8))),
        "lengths": draw_lengths(jax.random.fold_in(splits[6], 71), 0),
        "w_qkv": draw_w_qkv(jax.random.fold_in(splits[6], 71), 0),
        "w_out": normal_values(splits[3], (D, D), D ** -0.5, 0.1875, ((0, 64),)),
        "w_point": normal_values(splits[4], (D, D), D ** -0.5, 0.1875, ((0, 64),)),
        "w_depth": normal_values(splits[5], (KERNEL, D), KERNEL ** -0.5, 2.0, (), jnp.float32),
    }


def norm_rows(values):
    centre = lax.optimization_barrier(jnp.mean(values, axis=-1, keepdims=True))
    spread = lax.optimization_barrier(jnp.mean(jnp.square(values - centre), axis=-1, keepdims=True))
    return (values - centre) * lax.rsqrt(spread + 1e-05)

def attend(packed, length):
    total_rows = packed.shape[0]
    queries = packed[:, 0]
    keys_all = packed[:, 1]
    values_all = packed[:, 2]
    scaling = packed.shape[-1] ** (-0.5)
    block = min(512, total_rows)
    keep_mask = jnp.arange(total_rows) < length
    query_blocks = queries.reshape(total_rows // block, block, queries.shape[1], queries.shape[2])

    def one_block(qblock):
        scores = jnp.einsum('qnd,knd->nqk', qblock.astype(jnp.float32), keys_all.astype(jnp.float32)) * scaling
        scores = jnp.where(keep_mask[None, None, :], scores, -1e+30)
        highest = lax.optimization_barrier(jnp.max(scores, axis=-1, keepdims=True))
        powers = jnp.exp(scores - highest)
        totals = lax.optimization_barrier(jnp.sum(powers, axis=-1, keepdims=True))
        probs = (powers / totals).astype(jnp.bfloat16)
        mixed = jnp.einsum('nqk,knd->qnd', probs.astype(jnp.float32), values_all.astype(jnp.float32))
        return mixed.astype(jnp.bfloat16)
    return lax.map(one_block, query_blocks).reshape(total_rows, queries.shape[1], queries.shape[2])

def reference(frames, lengths, w_qkv, w_out, w_point, w_depth):
    margin = KERNEL // 2

    def layer_one(pair):
        signal, length = pair
        normed = norm_rows(signal.astype(jnp.float32)).astype(jnp.bfloat16)
        qkv = jnp.dot(normed, w_qkv, preferred_element_type=jnp.float32).astype(jnp.bfloat16)
        qkv = qkv.reshape(LEN, 3, HEADS, HDIM)
        attended = attend(qkv, length).reshape(LEN, D)
        projected = jnp.dot(attended, w_out, preferred_element_type=jnp.float32)
        resid = (signal.astype(jnp.float32) + projected).astype(jnp.bfloat16)
        valid = (jnp.arange(LEN) < length)[:, None]
        conv_in = jnp.where(valid, norm_rows(resid.astype(jnp.float32)), 0.0).astype(jnp.bfloat16)
        padded = jnp.pad(conv_in.astype(jnp.float32), ((margin, margin), (0, 0)))
        depth = jnp.zeros((LEN, D), jnp.float32)
        for offset in range(KERNEL):
            depth = depth + padded[offset:offset + LEN] * w_depth[offset]
        gated = (depth * jax.nn.sigmoid(depth)).astype(jnp.bfloat16)
        pointed = jnp.dot(gated, w_point, preferred_element_type=jnp.float32)
        return jnp.where(valid, resid.astype(jnp.float32) + pointed, 0.0).astype(jnp.bfloat16)
    return lax.map(layer_one, (frames, lengths))
```

```python
import jax
import jax.numpy as jnp
from jax import lax
from jax.experimental import pallas as pl
from jax.experimental.pallas import tpu as pltpu
from jax.sharding import PartitionSpec as P

D = 1024
HEADS = 8
KERNEL = 9
HDIM = 128
LEN = 512
HALO = 16
MESH = pl.DeviceIdType.MESH
LOG2E = 1.4426950408889634
N_SEM = 96


def norm_rows(values):
    centre = jnp.mean(values, axis=-1, keepdims=True)
    moved = values - centre
    spread = jnp.mean(jnp.square(moved), axis=-1, keepdims=True)
    return moved * lax.rsqrt(spread + 1e-05)


def kernel(
    len_ref, fr_ref, wq_ref, wo_ref, wp_ref, wd_ref, out_ref,
    NB, FH, BW, BO, BP, QKV, ATT, A, CV, ssem, rsem,
):
    s = lax.axis_index("seq")
    d = lax.axis_index("dp")
    y, c = s // 2, s % 2
    z, x = d // 4, d % 4
    j, r = z // 4, z % 4

    def at_z(k):
        return {"seq": s, "dp": lax.rem(z + k + 16, 16) * 4 + x}

    def at_x(k):
        return {"seq": s, "dp": z * 4 + lax.rem(x + k, 4)}

    def at_y(k):
        return {"seq": lax.rem(y + k, 4) * 2 + c, "dp": d}

    def at_s(k):
        return {"seq": lax.rem(s + k, 8), "dp": d}

    sibling = {"seq": y * 2 + 1 - c, "dp": d}

    started = []

    def copy(src, dst, device):
        n = len(started)
        made = pltpu.make_async_remote_copy(
            src_ref=src, dst_ref=dst, send_sem=ssem.at[n], recv_sem=rsem.at[n],
            device_id=device, device_id_type=MESH,
        )
        made.start()
        started.append(made)
        return made

    def same(ref, device):
        return copy(ref, ref, device)

    def arrived(copies):
        for one in copies:
            one.wait_recv()

    barrier = pltpu.get_barrier_semaphore()
    peers = [at_z(k) for k in (1, -1, 2, -2, 4, -4, 8)]
    peers += [at_x(k) for k in (1, 2, 3)] + [at_s(k) for k in range(1, 8)]
    for peer in peers:
        pl.semaphore_signal(barrier, inc=1, device_id=peer, device_id_type=MESH)

    def cols(ref, start, size):
        return ref[:, pl.ds(pl.multiple_of(start, 128), size)]

    def lanes(start, size):
        return pl.ds(pl.multiple_of(start, 128), size)

    for part in range(3):
        BW[j, r, x, :, part * 128 : part * 128 + 128] = cols(wq_ref, part * D + s * 128, 128)
    half = lanes(c * 512, 512)
    eighth = lanes(s * 128, 128)
    BO[j, r, x, :, half] = cols(wo_ref, c * 512, 512)
    BP[j, r, x, :, eighth] = cols(wp_ref, s * 128, 128)
    pl.semaphore_wait(barrier, len(peers))

    def hubs(ref):
        return [same(ref, at_z(k)) for k in (4, -4, 8)]

    def near(get):
        every, low, high = get(slice(None)), get(slice(0, 2)), get(slice(2, 4))
        return [same(every, at_z(1)), same(every, at_z(-1)), same(low, at_z(2)), same(high, at_z(-2))]

    def across(ref):
        return [same(ref, at_x(k)) for k in (1, 3, 2)]

    qk = slice(0, 256)
    vv = slice(256, 384)
    v1 = across(BW.at[j, r, x, :, vv])
    q1 = hubs(BW.at[j, r, x, :, qk])

    local = fr_ref[...].astype(jnp.float32)
    NB[:, s] = norm_rows(local).astype(jnp.bfloat16)
    own = NB.at[:, s]
    f1 = [same(own, at_y(1)), same(own, at_y(3)), same(own, sibling), same(own, at_y(2))]
    h1 = [
        copy(fr_ref.at[:, 64 - HALO : 64], FH.at[:, 0:HALO], at_s(1)),
        copy(fr_ref.at[:, 0:HALO], FH.at[:, 64 + HALO : 64 + 2 * HALO], at_s(7)),
    ]
    FH[:, HALO : 64 + HALO] = fr_ref[...]

    arrived(v1)
    v2 = hubs(BW.at[j, r, :, :, vv])
    arrived(q1)
    q2 = near(lambda js: BW.at[js, r, x, :, qk])
    p1 = hubs(BP.at[j, r, x, :, eighth])
    o1 = hubs(BO.at[j, r, x, :, half])
    arrived(v2)
    v3 = near(lambda js: BW.at[js, r, :, :, vv])
    arrived(q2)
    q3 = across(BW.at[:, :, x, :, qk])
    arrived(p1)
    p2 = near(lambda js: BP.at[js, r, x, :, eighth])
    arrived(o1)
    o2 = near(lambda js: BO.at[js, r, x, :, half])
    g1 = []
    for k, one in ((3, f1[0]), (1, f1[1]), (2, f1[3])):
        one.wait_recv()
        there = lax.rem(y + k, 4) * 2 + c
        g1.append(same(NB.at[:, there], sibling))
    arrived(p2)
    p3 = across(BP.at[:, :, x, :, eighth])
    arrived(q3)
    arrived(v3)
    arrived(o2)
    o3 = across(BO.at[:, :, x, :, half])
    k1 = [same(BO.at[:, :, x, :, half], sibling)]
    arrived([f1[2]])
    arrived(g1)

    weight = BW[...].reshape(D, 3 * HDIM)
    for rec in range(2):
        rows = NB[rec].reshape(LEN, D)
        QKV[rec] = jnp.dot(rows, weight, preferred_element_type=jnp.float32).astype(jnp.bfloat16)
    arrived(p3)
    p4 = [same(BP.at[:, :, :, :, eighth], at_y(k)) for k in (1, 3, 2)]
    k2 = [same(BP.at[:, :, :, :, eighth], sibling)]

    a1 = []
    zeros = jnp.zeros((2, HALO, HDIM), jnp.bfloat16)
    ATT[:, 0:HALO] = zeros
    ATT[:, LEN + HALO : LEN + 2 * HALO] = zeros
    key_at = lax.broadcasted_iota(jnp.int32, (128, LEN), 1)
    for rec in range(2):
        keep = key_at < len_ref[rec]
        keys = QKV[rec, :, HDIM : 2 * HDIM]
        vals = QKV[rec, :, 2 * HDIM : 3 * HDIM]
        for part in range(4):
            query = QKV[rec, part * 128 : part * 128 + 128, 0:HDIM]
            scores = lax.dot_general(
                query, keys, (((1,), (1,)), ((), ())), preferred_element_type=jnp.float32
            )
            scores = jnp.where(keep, scores, -1e30)
            highest = jnp.max(scores, axis=-1, keepdims=True)
            powers = jnp.exp2((scores - highest) * (LOG2E * HDIM**-0.5))
            totals = jnp.sum(powers, axis=-1, keepdims=True)
            mixed = jnp.dot(powers.astype(jnp.bfloat16), vals, preferred_element_type=jnp.float32)
            ATT[rec, HALO + part * 128 : HALO + part * 128 + 128] = (mixed / totals).astype(
                jnp.bfloat16
            )
        for k in (4, 3, 5, 2, 6, 1, 7):
            there = lax.rem(s + k, 8)
            src = ATT.at[rec, pl.ds(pl.multiple_of(there * 64, 64), 64 + 2 * HALO)]
            a1.append(copy(src, A.at[rec, :, eighth], at_s(k)))
        A[rec, :, eighth] = ATT[rec, pl.ds(pl.multiple_of(s * 64, 64), 64 + 2 * HALO)]

    for k, one in ((3, o3[0]), (1, o3[1]), (2, o3[2])):
        one.wait_recv()
        k1.append(same(BO.at[:, :, lax.rem(x + k, 4), :, half], sibling))
    for k, one in ((3, p4[0]), (1, p4[1]), (2, p4[2])):
        one.wait_recv()
        there = lanes((lax.rem(y + k, 4) * 2 + c) * 128, 128)
        k2.append(same(BP.at[:, :, :, :, there], sibling))
    arrived(h1)
    arrived(a1)
    arrived(k1)

    tall = 64 + 2 * HALO
    attended = A[...].reshape(2 * tall, D)
    projected = jnp.dot(attended, BO[...].reshape(D, D), preferred_element_type=jnp.float32)
    resid = (FH[...].astype(jnp.float32) + projected.reshape(2, tall, D)).astype(jnp.bfloat16)
    FH[...] = resid
    position = s * 64 - HALO + lax.broadcasted_iota(jnp.int32, (tall, 1), 0)
    inside = (position >= 0) & (position < LEN)
    for rec in range(2):
        valid = inside & (position < len_ref[rec])
        normed = jnp.where(valid, norm_rows(resid[rec].astype(jnp.float32)), 0.0)
        CV[rec] = normed.astype(jnp.bfloat16).astype(jnp.float32)
    gated = []
    for rec in range(2):
        depth = jnp.zeros((64, D), jnp.float32)
        for tap in range(KERNEL):
            start = HALO - KERNEL // 2 + tap
            depth = depth + CV[rec, start : start + 64] * wd_ref[tap : tap + 1]
        gated.append((depth * jax.nn.sigmoid(depth)).astype(jnp.bfloat16))
    gated = jnp.concatenate(gated, axis=0)
    arrived(k2)
    pointed = jnp.dot(gated, BP[...].reshape(D, D), preferred_element_type=jnp.float32)
    position = s * 64 + lax.broadcasted_iota(jnp.int32, (64, 1), 0)
    for rec in range(2):
        total = FH[rec, HALO : 64 + HALO].astype(jnp.float32) + pointed[rec * 64 : rec * 64 + 64]
        out_ref[rec] = jnp.where(position < len_ref[rec], total, 0.0).astype(jnp.bfloat16)
    for one in started:
        one.wait_send()


def body(frames, lengths, w_qkv, w_out, w_point, w_depth):
    vmem = pl.BlockSpec(memory_space=pltpu.VMEM)
    smem = pl.BlockSpec(memory_space=pltpu.SMEM)
    tall = 64 + 2 * HALO
    bf16 = jnp.bfloat16
    return pl.pallas_call(
        kernel,
        out_shape=jax.ShapeDtypeStruct((2, 64, D), bf16),
        in_specs=[smem, vmem, vmem, vmem, vmem, vmem],
        out_specs=vmem,
        scratch_shapes=[
            pltpu.VMEM((2, 8, 64, D), bf16),
            pltpu.VMEM((2, tall, D), bf16),
            pltpu.VMEM((4, 4, 4, 16, 3 * HDIM), bf16),
            pltpu.VMEM((4, 4, 4, 16, D), bf16),
            pltpu.VMEM((4, 4, 4, 16, D), bf16),
            pltpu.VMEM((2, LEN, 3 * HDIM), bf16),
            pltpu.VMEM((2, LEN + 2 * HALO, HDIM), bf16),
            pltpu.VMEM((2, tall, D), bf16),
            pltpu.VMEM((2, tall, D), jnp.float32),
            pltpu.SemaphoreType.DMA((N_SEM,)),
            pltpu.SemaphoreType.DMA((N_SEM,)),
        ],
        compiler_params=pltpu.CompilerParams(
            collective_id=0, has_side_effects=True, vmem_limit_bytes=48 << 20
        ),
        name="conformer",
    )(lengths, frames, w_qkv, w_out, w_point, w_depth)


def solution(mesh):
    in_specs = (P("dp", "seq", None), P("dp"), P("dp", None), P("dp", None), P("dp", None), P())
    out_specs = P("dp", "seq", None)
    return jax.shard_map(body, mesh=mesh, in_specs=in_specs, out_specs=out_specs, check_vma=False)
```

```python
import jax
import jax.numpy as jnp
from jax import lax
from jax.experimental import pallas as pl
from jax.experimental.pallas import tpu as pltpu
from jax.sharding import PartitionSpec as P

D = 1024
HEADS = 8
KERNEL = 9
HDIM = 128
LEN = 512
HALO = 16
MESH = pl.DeviceIdType.MESH
LOG2E = 1.4426950408889634
N_SEM = 160
WA = 128
RING_X = 0
RING_Y = 1
OA_AT = 2


def norm_rows(values):
    centre = jnp.mean(values, axis=-1, keepdims=True)
    moved = values - centre
    spread = jnp.mean(jnp.square(moved), axis=-1, keepdims=True)
    return moved * lax.rsqrt(spread + 1e-05)


def kernel(
    len_hbm, fr_ref, wq_ref, wo_ref, wp_ref, wd_hbm, out_ref,
    NB, FH, BW, BO, BP, QKV, ATT, A, CV, wd_ref, len_ref, ssem, rsem, lsem,
):
    s = lax.axis_index("seq")
    d = lax.axis_index("dp")
    y, c = s // 2, s % 2
    z, x = d // 4, d % 4

    def at_z(k):
        return {"seq": s, "dp": lax.rem(z + k + 16, 16) * 4 + x}

    def at_x(k):
        return {"seq": s, "dp": z * 4 + lax.rem(x + k, 4)}

    def at_y(k):
        return {"seq": lax.rem(y + k, 4) * 2 + c, "dp": d}

    def at_s(k):
        return {"seq": lax.rem(s + k, 8), "dp": d}

    sibling = {"seq": y * 2 + 1 - c, "dp": d}

    def lanes(start, size):
        return pl.ds(pl.multiple_of(start, 128), size)

    half = lanes(c * 512, 512)
    eighth = lanes(s * 128, 128)
    part_b, part_a = lanes(c * 512, 512 - WA), lanes(c * 512 + 512 - WA, WA)

    local = [(fr_ref, FH.at[:, HALO : 64 + HALO])]
    local += [
        (wq_ref.at[:, lanes(part * D + s * 128, 128)], BW.at[4, x, :, part * 128 : part * 128 + 128])
        for part in range(3)
    ]
    local += [
        (wp_ref.at[:, eighth], BP.at[4, x, :, eighth]),
        (wo_ref.at[:, half], BO.at[4, x, :, half]),
        (wd_hbm, wd_ref),
        (len_hbm, len_ref),
    ]
    local = [
        pltpu.make_async_copy(src, dst, lsem.at[i]) for i, (src, dst) in enumerate(local)
    ]
    for one in local:
        one.start()

    started = []

    def copy(src, dst, device):
        n = len(started)
        made = pltpu.make_async_remote_copy(
            src_ref=src, dst_ref=dst, send_sem=ssem.at[n], recv_sem=rsem.at[n],
            device_id=device, device_id_type=MESH,
        )
        made.start()
        started.append(made)
        return made

    def same(ref, device):
        return copy(ref, ref, device)

    def arrived(copies):
        for one in copies:
            one.wait_recv()

    barrier = pltpu.get_barrier_semaphore()
    peers = [at_z(k) for k in (4, -4, 3, -3, 2, -2, 1, -1)]
    peers += [at_x(k) for k in (2, 1, 3)] + [at_s(k) for k in (4, 3, 5, 2, 6, 1, 7)]
    for peer in peers:
        pl.semaphore_signal(barrier, inc=1, device_id=peer, device_id_type=MESH)
    for one in local:
        one.wait()
    pl.semaphore_wait(barrier, len(peers))

    def hubs(ref, at):
        own = at(ref, 4)
        return [copy(own, at(ref, 0), at_z(4)), copy(own, at(ref, 8), at_z(-4))]

    def near(ref, at):
        own = at(ref, 4)
        made = []
        for k in (3, 2, 1):
            made += [copy(own, at(ref, 4 - k), at_z(k)), copy(own, at(ref, 4 + k), at_z(-k))]
        return made

    def far(ref, at):
        low, high = at(ref, 0), at(ref, 8)
        made = [copy(at(ref, 8 * c), at(ref, 12), at_z(4 - 8 * c))]
        for k in (3, 2, 1):
            made += [copy(low, at(ref, 16 - k), at_z(k)), copy(high, at(ref, 8 + k), at_z(-k))]
        return made

    def across(ref):
        return [same(ref, at_x(k)) for k in (2, 1, 3)]

    slot = lambda ref, i: ref.at[i, x]
    slot_half = lambda ref, i: ref.at[i, x, :, part_b]
    slot_eighth = lambda ref, i: ref.at[i, x, :, eighth]
    slot_a = lambda ref, i: ref.at[i, :, :, part_a]
    NEAR, FAR = slice(0, 9), slice(9, 16)

    def ring(get, at, on=1):
        made = [same(get(0, 2), at(1)), same(get(0, 2), at(3))]
        return made if on else made + [same(get(0, 2), at(2))]

    def ring_on(get, at, first, on=1):
        first[0].wait_recv()
        made = [same(get(3, 0), at(1))] if on else [first[2]]
        first[1].wait_recv()
        return made + [same(get(1, 1), at(3))] if on else made

    def x_blocks(parts):
        return lambda k, part: BO.at[parts[part], lax.rem(x + k, 4), :, part_b]

    near_x = x_blocks((slice(0, 5), slice(5, 9), NEAR))
    far_x = x_blocks((slice(9, 12), slice(12, 16), FAR))

    def y_blocks(wave):
        parts = (slice(0, 2), slice(2, 4), slice(0, 4))
        return lambda k, part: BP.at[
            wave, parts[part], :, lanes((lax.rem(y + k, 4) * 2 + c) * 128, 128)
        ]

    near_y, far_y = y_blocks(NEAR), y_blocks(FAR)

    def frames_y(k, part):
        there = lax.rem(y + k, 4) * 2 + c
        return NB.at[part, there] if part < 2 else NB.at[:, there]

    oa0 = across(BO.at[4, x, :, part_a]) if WA else []
    oah, oan = [], []

    def oa_start(when):
        if WA and when == OA_AT:
            arrived(oa0)
            oah.extend(hubs(BO, slot_a))
            oan.extend(near(BO, slot_a))

    wh = hubs(BW, slot)
    wn = near(BW, slot)
    ph = hubs(BP, slot_eighth)
    oh = hubs(BO, slot_half)

    NB[:, s] = norm_rows(FH[:, HALO : 64 + HALO].astype(jnp.float32)).astype(jnp.bfloat16)
    f1 = ring(frames_y, at_y)
    f0 = [same(NB.at[:, s], sibling)]
    h1 = [
        copy(fr_ref.at[:, 64 - HALO : 64], FH.at[:, 0:HALO], at_s(1)),
        copy(fr_ref.at[:, 0:HALO], FH.at[:, 64 + HALO : 64 + 2 * HALO], at_s(7)),
    ]

    arrived(wh)
    wf = far(BW, slot)
    pn = near(BP, slot_eighth)
    on = near(BO, slot_half)
    arrived(wn)
    wxn = across(BW.at[NEAR, x])
    arrived(ph)
    pf = far(BP, slot_eighth)
    arrived(oh)
    of = far(BO, slot_half)
    oa_start(0)
    arrived(pn)
    pxn = across(BP.at[NEAR, x, :, eighth])
    arrived(wf)
    wxf = across(BW.at[FAR, x])
    oa_start(1)
    f2 = ring_on(frames_y, at_y, f1)
    g1 = [same(frames_y(k, 2), sibling) for k in (1, 3)]
    arrived(pf)
    pxf = across(BP.at[FAR, x, :, eighth])
    arrived(on)
    oxn = ring(near_x, at_x, RING_X)
    arrived(of)
    oxf = ring(far_x, at_x, RING_X)
    k1 = [same(BO.at[:, x, :, part_b], sibling)]
    oa_start(2)
    arrived(pxn)
    pyn = ring(near_y, at_y, RING_Y)
    arrived(f2)
    g1 += [same(frames_y(2, 2), sibling)]
    arrived(wxn)
    arrived(f0)
    arrived(g1)
    arrived(wxf)

    def natural(ref):
        planes = [ref[lax.rem(i - z + 20, 16)] for i in range(16)]
        return jnp.concatenate([p.reshape(64, p.shape[-1]) for p in planes], axis=0)

    weight = natural(BW)
    for rec in range(2):
        rows = NB[rec].reshape(LEN, D)
        QKV[rec] = jnp.dot(rows, weight, preferred_element_type=jnp.float32).astype(jnp.bfloat16)
    if WA:
        arrived(oah)
        oaf = far(BO, slot_a)
    arrived(pxf)
    pyf = ring(far_y, at_y, RING_Y)
    k2 = [same(BP.at[:, :, :, eighth], sibling)]

    a1 = []
    zeros = jnp.zeros((2, HALO, HDIM), jnp.bfloat16)
    ATT[:, 0:HALO] = zeros
    ATT[:, LEN + HALO : LEN + 2 * HALO] = zeros
    key_at = lax.broadcasted_iota(jnp.int32, (128, LEN), 1)

    def attention(rec):
        keep = key_at < len_ref[rec]
        keys = QKV[rec, :, HDIM : 2 * HDIM]
        vals = QKV[rec, :, 2 * HDIM : 3 * HDIM]
        for part in range(4):
            query = QKV[rec, part * 128 : part * 128 + 128, 0:HDIM]
            scores = lax.dot_general(
                query, keys, (((1,), (1,)), ((), ())), preferred_element_type=jnp.float32
            )
            scores = jnp.where(keep, scores, -1e30)
            highest = jnp.max(scores, axis=-1, keepdims=True)
            powers = jnp.exp2((scores - highest) * (LOG2E * HDIM**-0.5))
            totals = jnp.sum(powers, axis=-1, keepdims=True)
            mixed = jnp.dot(powers.astype(jnp.bfloat16), vals, preferred_element_type=jnp.float32)
            ATT[rec, HALO + part * 128 : HALO + part * 128 + 128] = (mixed / totals).astype(
                jnp.bfloat16
            )
        made = []
        for k in (4, 3, 5, 2, 6, 1, 7):
            there = lax.rem(s + k, 8)
            src = ATT.at[rec, pl.ds(pl.multiple_of(there * 64, 64), 64 + 2 * HALO)]
            made += [copy(src, A.at[rec, :, eighth], at_s(k))]
        A[rec, :, eighth] = ATT[rec, pl.ds(pl.multiple_of(s * 64, 64), 64 + 2 * HALO)]
        return made

    a1 += attention(0)
    oxn2 = ring_on(near_x, at_x, oxn, RING_X)
    k1 += [same(near_x(k, 2), sibling) for k in (1, 3)]
    a1 += attention(1)
    oxf2 = ring_on(far_x, at_x, oxf, RING_X)
    k1 += [same(far_x(k, 2), sibling) for k in (1, 3)]
    if WA:
        arrived(oan)
        k1 += [same(slot_a(BO, NEAR), sibling)]
    pyn2 = ring_on(near_y, at_y, pyn, RING_Y)
    k2 += [same(near_y(k, 2), sibling) for k in (1, 3)]
    arrived(oxn2)
    k1 += [same(near_x(2, 2), sibling)]
    arrived(oxf2)
    k1 += [same(far_x(2, 2), sibling)]
    if WA:
        arrived(oaf)
        k1 += [same(slot_a(BO, FAR), sibling)]
    pyf2 = ring_on(far_y, at_y, pyf, RING_Y)
    k2 += [same(far_y(k, 2), sibling) for k in (1, 3)]
    arrived(pyn2)
    k2 += [same(near_y(2, 2), sibling)]
    arrived(pyf2)
    k2 += [same(far_y(2, 2), sibling)]
    arrived(h1)
    arrived(a1)
    arrived(k1)

    tall = 64 + 2 * HALO
    attended = A[...].reshape(2 * tall, D)
    projected = jnp.dot(attended, natural(BO), preferred_element_type=jnp.float32)
    resid = (FH[...].astype(jnp.float32) + projected.reshape(2, tall, D)).astype(jnp.bfloat16)
    FH[...] = resid
    position = s * 64 - HALO + lax.broadcasted_iota(jnp.int32, (tall, 1), 0)
    inside = (position >= 0) & (position < LEN)
    for rec in range(2):
        valid = inside & (position < len_ref[rec])
        normed = jnp.where(valid, norm_rows(resid[rec].astype(jnp.float32)), 0.0)
        CV[rec] = normed.astype(jnp.bfloat16).astype(jnp.float32)
    gated = []
    for rec in range(2):
        depth = jnp.zeros((64, D), jnp.float32)
        for tap in range(KERNEL):
            start = HALO - KERNEL // 2 + tap
            depth = depth + CV[rec, start : start + 64] * wd_ref[tap : tap + 1]
        gated.append((depth * jax.nn.sigmoid(depth)).astype(jnp.bfloat16))
    gated = jnp.concatenate(gated, axis=0)
    arrived(k2)
    pointed = jnp.dot(gated, natural(BP), preferred_element_type=jnp.float32)
    position = s * 64 + lax.broadcasted_iota(jnp.int32, (64, 1), 0)
    for rec in range(2):
        total = FH[rec, HALO : 64 + HALO].astype(jnp.float32) + pointed[rec * 64 : rec * 64 + 64]
        out_ref[rec] = jnp.where(position < len_ref[rec], total, 0.0).astype(jnp.bfloat16)
    for one in started:
        one.wait_send()


def body(frames, lengths, w_qkv, w_out, w_point, w_depth):
    vmem = pl.BlockSpec(memory_space=pltpu.VMEM)
    hbm = pl.BlockSpec(memory_space=pltpu.HBM)
    tall = 64 + 2 * HALO
    bf16 = jnp.bfloat16
    return pl.pallas_call(
        kernel,
        out_shape=jax.ShapeDtypeStruct((2, 64, D), bf16),
        in_specs=[hbm] * 6,
        out_specs=vmem,
        scratch_shapes=[
            pltpu.VMEM((2, 8, 64, D), bf16),
            pltpu.VMEM((2, tall, D), bf16),
            pltpu.VMEM((16, 4, 16, 3 * HDIM), bf16),
            pltpu.VMEM((16, 4, 16, D), bf16),
            pltpu.VMEM((16, 4, 16, D), bf16),
            pltpu.VMEM((2, LEN, 3 * HDIM), bf16),
            pltpu.VMEM((2, LEN + 2 * HALO, HDIM), bf16),
            pltpu.VMEM((2, tall, D), bf16),
            pltpu.VMEM((2, tall, D), jnp.float32),
            pltpu.VMEM((KERNEL, D), jnp.float32),
            pltpu.SMEM((2,), jnp.int32),
            pltpu.SemaphoreType.DMA((N_SEM,)),
            pltpu.SemaphoreType.DMA((N_SEM,)),
            pltpu.SemaphoreType.DMA((8,)),
        ],
        compiler_params=pltpu.CompilerParams(
            collective_id=0, has_side_effects=True, vmem_limit_bytes=61 << 20
        ),
        name="conformer",
    )(lengths, frames, w_qkv, w_out, w_point, w_depth)


def solution(mesh):
    in_specs = (P("dp", "seq", None), P("dp"), P("dp", None), P("dp", None), P("dp", None), P())
    out_specs = P("dp", "seq", None)
    return jax.shard_map(body, mesh=mesh, in_specs=in_specs, out_specs=out_specs, check_vma=False)
```

```python
import jax
import jax.numpy as jnp
from jax import lax
from jax.experimental import pallas as pl
from jax.experimental.pallas import tpu as pltpu
from jax.sharding import PartitionSpec as P

D = 1024
HEADS = 8
KERNEL = 9
HDIM = 128
LEN = 512
HALO = 16
MESH = pl.DeviceIdType.MESH
LOG2E = 1.4426950408889634
N_SEM = 160
WA = 128
RING_Y = 1
O_AT = 0
OF_AT = 1
OXN_AT = 2
OA_AT = 1
PX = 1


def norm_rows(values):
    centre = jnp.mean(values, axis=-1, keepdims=True)
    moved = values - centre
    spread = jnp.mean(jnp.square(moved), axis=-1, keepdims=True)
    return moved * lax.rsqrt(spread + 1e-05)


def kernel(
    len_hbm, fr_ref, wq_ref, wo_ref, wp_ref, wd_hbm, out_ref,
    NB, FH, BW, BO, BP, QKV, ATT, A, CV, wd_ref, len_ref, ssem, rsem, lsem,
):
    s = lax.axis_index("seq")
    d = lax.axis_index("dp")
    y, c = s // 2, s % 2
    z, x = d // 4, d % 4

    def at_z(k):
        return {"seq": s, "dp": lax.rem(z + k + 16, 16) * 4 + x}

    def at_x(k):
        return {"seq": s, "dp": z * 4 + lax.rem(x + k, 4)}

    def at_y(k):
        return {"seq": lax.rem(y + k, 4) * 2 + c, "dp": d}

    def at_s(k):
        return {"seq": lax.rem(s + k, 8), "dp": d}

    sibling = {"seq": y * 2 + 1 - c, "dp": d}

    def lanes(start, size):
        return pl.ds(pl.multiple_of(start, 128), size)

    half = lanes(c * 512, 512)
    eighth = lanes(s * 128, 128)
    part_b, part_a = lanes(c * 512, 512 - WA), lanes(c * 512 + 512 - WA, WA)

    started = []

    def copy(src, dst, device):
        n = len(started)
        made = pltpu.make_async_remote_copy(
            src_ref=src, dst_ref=dst, send_sem=ssem.at[n], recv_sem=rsem.at[n],
            device_id=device, device_id_type=MESH,
        )
        made.start()
        started.append(made)
        return made

    def same(ref, device):
        return copy(ref, ref, device)

    def arrived(copies):
        for one in copies:
            one.wait_recv()

    barrier = pltpu.get_barrier_semaphore()
    peers = [at_z(k) for k in (4, -4, 3, -3, 2, -2, 1, -1)]
    peers += [at_x(k) for k in (2, 1, 3)] + [at_s(k) for k in (4, 3, 5, 2, 6, 1, 7)]
    for peer in peers:
        pl.semaphore_signal(barrier, inc=1, device_id=peer, device_id_type=MESH)
    local = [(fr_ref, FH.at[:, HALO : 64 + HALO])]
    local += [
        (wq_ref.at[:, lanes(part * D + s * 128, 128)], BW.at[4, x, :, part * 128 : part * 128 + 128])
        for part in range(3)
    ]
    local += [
        (wp_ref.at[:, eighth], BP.at[4, x, :, eighth]),
        (wo_ref.at[:, half], BO.at[4, x, :, half]),
        (wd_hbm, wd_ref),
        (len_hbm, len_ref),
    ]
    local = [
        pltpu.make_async_copy(src, dst, lsem.at[i]) for i, (src, dst) in enumerate(local)
    ]
    for one in local:
        one.start()

    for one in local[1:]:
        one.wait()
    pl.semaphore_wait(barrier, len(peers))

    def hubs(ref, at):
        own = at(ref, 4)
        return [copy(own, at(ref, 0), at_z(4)), copy(own, at(ref, 8), at_z(-4))]

    def near(ref, at):
        own = at(ref, 4)
        made = []
        for k in (3, 2, 1):
            made += [copy(own, at(ref, 4 - k), at_z(k)), copy(own, at(ref, 4 + k), at_z(-k))]
        return made

    def far(ref, at):
        low, high = at(ref, 0), at(ref, 8)
        made = [copy(at(ref, 8 * c), at(ref, 12), at_z(4 - 8 * c))]
        for k in (3, 2, 1):
            made += [copy(low, at(ref, 16 - k), at_z(k)), copy(high, at(ref, 8 + k), at_z(-k))]
        return made

    def across(ref):
        return [same(ref, at_x(k)) for k in (2, 1, 3)]

    slot = lambda ref, i: ref.at[i, x]
    slot_half = lambda ref, i: ref.at[i, x, :, part_b]
    slot_eighth = lambda ref, i: ref.at[i, x, :, eighth]
    slot_a = lambda ref, i: ref.at[i, :, :, part_a]
    NEAR, FAR = slice(0, 9), slice(9, 16)

    def ring(get, at, on=1):
        made = [same(get(0, 2), at(1)), same(get(0, 2), at(3))]
        return made if on else made + [same(get(0, 2), at(2))]

    def ring_on(get, at, first, on=1):
        first[0].wait_recv()
        made = [same(get(3, 0), at(1))] if on else [first[2]]
        first[1].wait_recv()
        return made + [same(get(1, 1), at(3))] if on else made

    def x_blocks(parts):
        return lambda k, part: BO.at[parts[part], lax.rem(x + k, 4), :, part_b]

    near_x = x_blocks((slice(0, 5), slice(5, 9), NEAR))
    far_x = x_blocks((slice(9, 12), slice(12, 16), FAR))

    def y_blocks(wave):
        parts = (slice(0, 2), slice(2, 4), slice(0, 4))
        return lambda k, part: BP.at[
            wave, parts[part], :, lanes((lax.rem(y + k, 4) * 2 + c) * 128, 128)
        ]

    near_y, far_y = y_blocks(NEAR), y_blocks(FAR)

    def frames_y(k, part):
        there = lax.rem(y + k, 4) * 2 + c
        return NB.at[part, there] if part < 2 else NB.at[:, there]

    oa0 = across(BO.at[4, x, :, part_a]) if WA else []
    wh = hubs(BW, slot)
    wn = near(BW, slot)
    ph = hubs(BP, slot_eighth)

    local[0].wait()
    NB[:, s] = norm_rows(FH[:, HALO : 64 + HALO].astype(jnp.float32)).astype(jnp.bfloat16)

    def frames(k, rec):
        return NB.at[rec, lax.rem(y + k, 4) * 2 + c]

    f1 = [same(frames(0, 0), at_y(1)), same(frames(0, 1), at_y(3))]
    f1 += [same(frames(0, 1), at_y(1)), same(frames(0, 0), at_y(3))]
    f0 = [same(NB.at[:, s], sibling)]
    h1 = [
        copy(fr_ref.at[:, 64 - HALO : 64], FH.at[:, 0:HALO], at_s(1)),
        copy(fr_ref.at[:, 0:HALO], FH.at[:, 64 + HALO : 64 + 2 * HALO], at_s(7)),
    ]
    pn = near(BP, slot_eighth)

    arrived(wh)
    wf = far(BW, slot)
    arrived(ph)
    pf = far(BP, slot_eighth)
    arrived(wn)
    wxn = across(BW.at[NEAR, x])
    oh, on, of, oxn, oxf, oah, oan = [], [], [], [], [], [], []

    def o_start(when):
        if when == O_AT:
            oh.extend(hubs(BO, slot_half))
            on.extend(near(BO, slot_half))

    def oa_start(when):
        if WA and when == OA_AT:
            arrived(oa0)
            oah.extend(hubs(BO, slot_a))
            oan.extend(near(BO, slot_a))

    def of_start(when):
        if when == OF_AT:
            arrived(oh)
            of.extend(far(BO, slot_half))

    def oxn_start(when):
        if when == OXN_AT:
            arrived(on)
            oxn.extend(ring(near_x, at_x, 0))

    o_start(0)
    arrived(f1[0:2])
    f2 = [same(frames(3, 0), at_y(1)), same(frames(1, 1), at_y(3))]
    if PX == 0:
        arrived(pn)
        pxn = across(BP.at[NEAR, x, :, eighth])
    o_start(1)
    of_start(0)
    arrived(wf)
    wxf = across(BW.at[FAR, x])
    o_start(2)
    if PX == 1:
        arrived(pn)
        pxn = across(BP.at[NEAR, x, :, eighth])
    arrived(f1[2:4])
    g1 = [same(NB.at[:, lax.rem(y + k, 4) * 2 + c], sibling) for k in (1, 3)]
    arrived(pf)
    pxf = across(BP.at[FAR, x, :, eighth])
    of_start(1)
    oxn_start(0)
    oa_start(1)
    arrived(f2)
    g1 += [same(NB.at[:, lax.rem(y + 2, 4) * 2 + c], sibling)]
    arrived(wxn)
    arrived(f0)
    arrived(g1)
    arrived(wxf)
    of_start(2)
    oxn_start(1)

    def natural(ref):
        planes = [ref[lax.rem(i - z + 20, 16)] for i in range(16)]
        return jnp.concatenate([p.reshape(64, p.shape[-1]) for p in planes], axis=0)

    weight = natural(BW)
    for rec in range(2):
        rows = NB[rec].reshape(LEN, D)
        qkv = jnp.dot(rows, weight, preferred_element_type=jnp.float32)
        QKV[rec, HALO : LEN + HALO] = qkv.astype(jnp.bfloat16)
        if rec == 0:
            arrived(pxn)
            pyn = ring(near_y, at_y, RING_Y)
    arrived(pxf)
    pyf = ring(far_y, at_y, RING_Y)
    k2 = [same(BP.at[:, :, :, eighth], sibling)]
    oxn_start(2)
    arrived(of)
    oxf += ring(far_x, at_x, 0)
    k1 = [same(BO.at[:, x, :, part_b], sibling)]
    oaf = []
    if WA:
        arrived(oah)
        oaf = far(BO, slot_a)

    zeros = jnp.zeros((2, HALO, HDIM), jnp.bfloat16)
    QKV[:, 0:HALO, 0:HDIM] = zeros
    QKV[:, LEN + HALO : LEN + 2 * HALO, 0:HDIM] = zeros
    tall = 64 + 2 * HALO
    wide = 128 + 2 * HALO
    key_at = lax.broadcasted_iota(jnp.int32, (wide // 2, LEN), 1)

    def attention(k):
        chip = lax.rem(y + k, 4)
        for rec in range(2):
            keep = key_at < len_ref[rec]
            keys = QKV[rec, HALO : LEN + HALO, HDIM : 2 * HDIM]
            vals = QKV[rec, HALO : LEN + HALO, 2 * HDIM : 3 * HDIM]
            for part in range(2):
                first = pl.multiple_of(chip * 128 + part * (wide // 2), 16)
                query = QKV[rec, pl.ds(first, wide // 2), 0:HDIM]
                scores = lax.dot_general(
                    query, keys, (((1,), (1,)), ((), ())), preferred_element_type=jnp.float32
                )
                scores = jnp.where(keep, scores, -1e30)
                highest = jnp.max(scores, axis=-1, keepdims=True)
                powers = jnp.exp2((scores - highest) * (LOG2E * HDIM**-0.5))
                totals = jnp.sum(powers, axis=-1, keepdims=True)
                mixed = jnp.dot(
                    powers.astype(jnp.bfloat16), vals, preferred_element_type=jnp.float32
                )
                ATT[k, rec, part * (wide // 2) : (part + 1) * (wide // 2)] = (
                    mixed / totals
                ).astype(jnp.bfloat16)
        made = []
        for other in (0, 1):
            core = lax.rem(c + other, 2)
            rows = pl.ds(pl.multiple_of(core * 64, 64), tall)
            if k or other:
                device = {"seq": chip * 2 + core, "dp": d}
                made.append(copy(ATT.at[k, :, rows], A.at[:, :, eighth], device))
            else:
                A[:, :, eighth] = ATT[k, :, rows]
        return made

    a1 = attention(2) + attention(1)
    pyn2 = ring_on(near_y, at_y, pyn, RING_Y)
    k2 += [same(near_y(k, 2), sibling) for k in (1, 3)]
    a1 += attention(3) + attention(0)
    ring_on(near_x, at_x, oxn, 0)
    k1 += [same(near_x(k, 2), sibling) for k in (1, 3)]
    if WA:
        arrived(oan)
        k1 += [same(slot_a(BO, NEAR), sibling)]
    pyf2 = ring_on(far_y, at_y, pyf, RING_Y)
    k2 += [same(far_y(k, 2), sibling) for k in (1, 3)]
    arrived(oxn[2:])
    k1 += [same(near_x(2, 2), sibling)]
    ring_on(far_x, at_x, oxf, 0)
    k1 += [same(far_x(k, 2), sibling) for k in (1, 3)]
    arrived(oxf[2:])
    k1 += [same(far_x(2, 2), sibling)]
    if WA:
        arrived(oaf)
        k1 += [same(slot_a(BO, FAR), sibling)]
    arrived(h1)
    arrived(a1)
    arrived(k1)

    attended = A[...].reshape(2 * tall, D)
    projected = jnp.dot(attended, natural(BO), preferred_element_type=jnp.float32)
    resid = (FH[...].astype(jnp.float32) + projected.reshape(2, tall, D)).astype(jnp.bfloat16)
    FH[...] = resid
    position = s * 64 - HALO + lax.broadcasted_iota(jnp.int32, (tall, 1), 0)
    inside = (position >= 0) & (position < LEN)
    for rec in range(2):
        valid = inside & (position < len_ref[rec])
        normed = jnp.where(valid, norm_rows(resid[rec].astype(jnp.float32)), 0.0)
        CV[rec] = normed.astype(jnp.bfloat16).astype(jnp.float32)
    arrived(pyn2)
    k2 += [same(near_y(2, 2), sibling)]
    arrived(pyf2)
    k2 += [same(far_y(2, 2), sibling)]
    gated = []
    for rec in range(2):
        depth = jnp.zeros((64, D), jnp.float32)
        for tap in range(KERNEL):
            start = HALO - KERNEL // 2 + tap
            depth = depth + CV[rec, start : start + 64] * wd_ref[tap : tap + 1]
        gated.append((depth * jax.nn.sigmoid(depth)).astype(jnp.bfloat16))
    gated = jnp.concatenate(gated, axis=0)
    arrived(k2)
    pointed = jnp.dot(gated, natural(BP), preferred_element_type=jnp.float32)
    position = s * 64 + lax.broadcasted_iota(jnp.int32, (64, 1), 0)
    for rec in range(2):
        total = FH[rec, HALO : 64 + HALO].astype(jnp.float32) + pointed[rec * 64 : rec * 64 + 64]
        out_ref[rec] = jnp.where(position < len_ref[rec], total, 0.0).astype(jnp.bfloat16)
    for one in started:
        one.wait_send()


def body(frames, lengths, w_qkv, w_out, w_point, w_depth):
    vmem = pl.BlockSpec(memory_space=pltpu.VMEM)
    hbm = pl.BlockSpec(memory_space=pltpu.HBM)
    tall = 64 + 2 * HALO
    bf16 = jnp.bfloat16
    return pl.pallas_call(
        kernel,
        out_shape=jax.ShapeDtypeStruct((2, 64, D), bf16),
        in_specs=[hbm] * 6,
        out_specs=vmem,
        scratch_shapes=[
            pltpu.VMEM((2, 8, 64, D), bf16),
            pltpu.VMEM((2, tall, D), bf16),
            pltpu.VMEM((16, 4, 16, 3 * HDIM), bf16),
            pltpu.VMEM((16, 4, 16, D), bf16),
            pltpu.VMEM((16, 4, 16, D), bf16),
            pltpu.VMEM((2, LEN + 2 * HALO, 3 * HDIM), bf16),
            pltpu.VMEM((4, 2, 128 + 2 * HALO, HDIM), bf16),
            pltpu.VMEM((2, tall, D), bf16),
            pltpu.VMEM((2, tall, D), jnp.float32),
            pltpu.VMEM((KERNEL, D), jnp.float32),
            pltpu.SMEM((2,), jnp.int32),
            pltpu.SemaphoreType.DMA((N_SEM,)),
            pltpu.SemaphoreType.DMA((N_SEM,)),
            pltpu.SemaphoreType.DMA((8,)),
        ],
        compiler_params=pltpu.CompilerParams(
            collective_id=0, has_side_effects=True, vmem_limit_bytes=61 << 20
        ),
        name="conformer",
    )(lengths, frames, w_qkv, w_out, w_point, w_depth)


def solution(mesh):
    in_specs = (P("dp", "seq", None), P("dp"), P("dp", None), P("dp", None), P("dp", None), P())
    out_specs = P("dp", "seq", None)
    return jax.shard_map(body, mesh=mesh, in_specs=in_specs, out_specs=out_specs, check_vma=False)
```

```python
import jax
import jax.numpy as jnp
from jax import lax
from jax.experimental import pallas as pl
from jax.experimental.pallas import tpu as pltpu
from jax.sharding import PartitionSpec as P

D = 1024
HEADS = 8
KERNEL = 9
HDIM = 128
LEN = 512
HALO = 16
MESH = pl.DeviceIdType.MESH
LOG2E = 1.4426950408889634
N_SEM = 160
WA = 128
RING_Y = 1
O_AT = 1
OF_AT = 1
OXN_AT = 2
OA_AT = 1
PX = 1


def norm_rows(values):
    centre = jnp.mean(values, axis=-1, keepdims=True)
    moved = values - centre
    spread = jnp.mean(jnp.square(moved), axis=-1, keepdims=True)
    return moved * lax.rsqrt(spread + 1e-05)


def kernel(
    len_hbm, fr_ref, wq_ref, wo_ref, wp_ref, wd_hbm, out_ref,
    NB, FH, BW, BO, BP, QKV, ATT, A, CV, wd_ref, len_ref, ssem, rsem, lsem,
):
    s = lax.axis_index("seq")
    d = lax.axis_index("dp")
    y, c = s // 2, s % 2
    z, x = d // 4, d % 4

    def at_z(k):
        return {"seq": s, "dp": lax.rem(z + k + 16, 16) * 4 + x}

    def at_x(k):
        return {"seq": s, "dp": z * 4 + lax.rem(x + k, 4)}

    def at_y(k):
        return {"seq": lax.rem(y + k, 4) * 2 + c, "dp": d}

    def at_s(k):
        return {"seq": lax.rem(s + k, 8), "dp": d}

    sibling = {"seq": y * 2 + 1 - c, "dp": d}

    def lanes(start, size):
        return pl.ds(pl.multiple_of(start, 128), size)

    half = lanes(c * 512, 512)
    eighth = lanes(s * 128, 128)
    part_b, part_a = lanes(c * 512, 512 - WA), lanes(c * 512 + 512 - WA, WA)

    started = []

    def copy(src, dst, device):
        n = len(started)
        made = pltpu.make_async_remote_copy(
            src_ref=src, dst_ref=dst, send_sem=ssem.at[n], recv_sem=rsem.at[n],
            device_id=device, device_id_type=MESH,
        )
        made.start()
        started.append(made)
        return made

    def same(ref, device):
        return copy(ref, ref, device)

    def arrived(copies):
        for one in copies:
            one.wait_recv()

    barrier = pltpu.get_barrier_semaphore()
    peers = [at_z(k) for k in (4, -4, 3, -3, 2, -2, 1, -1)]
    peers += [at_x(k) for k in (2, 1, 3)] + [at_s(k) for k in (4, 3, 5, 2, 6, 1, 7)]
    for peer in peers:
        pl.semaphore_signal(barrier, inc=1, device_id=peer, device_id_type=MESH)
    local = [(fr_ref, FH.at[:, HALO : 64 + HALO])]
    local += [
        (wq_ref.at[:, lanes(part * D + s * 128, 128)], BW.at[4, x, :, part * 128 : part * 128 + 128])
        for part in range(3)
    ]
    local += [
        (wp_ref.at[:, eighth], BP.at[4, x, :, eighth]),
        (wo_ref.at[:, half], BO.at[4, x, :, half]),
        (wd_hbm, wd_ref),
        (len_hbm, len_ref),
    ]
    local = [
        pltpu.make_async_copy(src, dst, lsem.at[i]) for i, (src, dst) in enumerate(local)
    ]
    for one in local:
        one.start()

    for one in local[1:]:
        one.wait()
    pl.semaphore_wait(barrier, len(peers))

    def hubs(ref, at):
        own = at(ref, 4)
        return [copy(own, at(ref, 0), at_z(4)), copy(own, at(ref, 8), at_z(-4))]

    def near(ref, at):
        own = at(ref, 4)
        made = []
        for k in (3, 2, 1):
            made += [copy(own, at(ref, 4 - k), at_z(k)), copy(own, at(ref, 4 + k), at_z(-k))]
        return made

    def far(ref, at):
        low, high = at(ref, 0), at(ref, 8)
        made = [copy(at(ref, 8 * c), at(ref, 12), at_z(4 - 8 * c))]
        for k in (3, 2, 1):
            made += [copy(low, at(ref, 16 - k), at_z(k)), copy(high, at(ref, 8 + k), at_z(-k))]
        return made

    def across(ref):
        return [same(ref, at_x(k)) for k in (2, 1, 3)]

    slot = lambda ref, i: ref.at[i, x]
    slot_half = lambda ref, i: ref.at[i, x, :, part_b]
    slot_eighth = lambda ref, i: ref.at[i, x, :, eighth]
    slot_a = lambda ref, i: ref.at[i, :, :, part_a]
    NEAR, FAR = slice(0, 9), slice(9, 16)

    def ring(get, at, on=1):
        made = [same(get(0, 2), at(1)), same(get(0, 2), at(3))]
        return made if on else made + [same(get(0, 2), at(2))]

    def ring_on(get, at, first, on=1):
        first[0].wait_recv()
        made = [same(get(3, 0), at(1))] if on else [first[2]]
        first[1].wait_recv()
        return made + [same(get(1, 1), at(3))] if on else made

    def x_blocks(parts):
        return lambda k, part: BO.at[parts[part], lax.rem(x + k, 4), :, part_b]

    near_x = x_blocks((slice(0, 5), slice(5, 9), NEAR))
    far_x = x_blocks((slice(9, 12), slice(12, 16), FAR))

    def y_blocks(wave):
        parts = (slice(0, 2), slice(2, 4), slice(0, 4))
        return lambda k, part: BP.at[
            wave, parts[part], :, lanes((lax.rem(y + k, 4) * 2 + c) * 128, 128)
        ]

    near_y, far_y = y_blocks(NEAR), y_blocks(FAR)

    def frames_y(k, part):
        there = lax.rem(y + k, 4) * 2 + c
        return NB.at[part, there] if part < 2 else NB.at[:, there]

    oa0 = across(BO.at[4, x, :, part_a]) if WA else []
    wh = hubs(BW, slot)
    wn = near(BW, slot)
    ph = hubs(BP, slot_eighth)

    local[0].wait()
    NB[:, s] = norm_rows(FH[:, HALO : 64 + HALO].astype(jnp.float32)).astype(jnp.bfloat16)

    def frames(k, rec):
        return NB.at[rec, lax.rem(y + k, 4) * 2 + c]

    f1 = [same(frames(0, 0), at_y(1)), same(frames(0, 1), at_y(3))]
    f1 += [same(frames(0, 1), at_y(1)), same(frames(0, 0), at_y(3))]
    f0 = [same(NB.at[:, s], sibling)]
    h1 = [
        copy(fr_ref.at[:, 64 - HALO : 64], FH.at[:, 0:HALO], at_s(1)),
        copy(fr_ref.at[:, 0:HALO], FH.at[:, 64 + HALO : 64 + 2 * HALO], at_s(7)),
    ]
    pn = near(BP, slot_eighth)

    arrived(wh)
    wf = far(BW, slot)
    arrived(ph)
    pf = far(BP, slot_eighth)
    arrived(wn)
    wxn = across(BW.at[NEAR, x])
    oh, on, of, oxn, oxf, oah, oan = [], [], [], [], [], [], []

    def o_start(when):
        if when == O_AT:
            oh.extend(hubs(BO, slot_half))
            on.extend(near(BO, slot_half))

    def oa_start(when):
        if WA and when == OA_AT:
            arrived(oa0)
            oah.extend(hubs(BO, slot_a))
            oan.extend(near(BO, slot_a))

    def of_start(when):
        if when == OF_AT:
            arrived(oh)
            of.extend(far(BO, slot_half))

    def oxn_start(when):
        if when == OXN_AT:
            arrived(on)
            oxn.extend(ring(near_x, at_x, 0))

    o_start(0)
    arrived(f1[0:2])
    f2 = [same(frames(3, 0), at_y(1)), same(frames(1, 1), at_y(3))]
    if PX == 0:
        arrived(pn)
        pxn = across(BP.at[NEAR, x, :, eighth])
    o_start(1)
    of_start(0)
    arrived(wf)
    wxf = across(BW.at[FAR, x])
    o_start(2)
    if PX == 1:
        arrived(pn)
        pxn = across(BP.at[NEAR, x, :, eighth])
    arrived(f1[2:4])
    g1 = [same(NB.at[:, lax.rem(y + k, 4) * 2 + c], sibling) for k in (1, 3)]
    arrived(pf)
    pxf = across(BP.at[FAR, x, :, eighth])
    of_start(1)
    oxn_start(0)
    oa_start(1)
    arrived(f2)
    g1 += [same(NB.at[:, lax.rem(y + 2, 4) * 2 + c], sibling)]
    arrived(wxn)
    arrived(f0)
    arrived(g1)
    arrived(wxf)
    of_start(2)
    oxn_start(1)

    def natural(ref):
        planes = [ref[lax.rem(i - z + 20, 16)] for i in range(16)]
        return jnp.concatenate([p.reshape(64, p.shape[-1]) for p in planes], axis=0)

    weight = natural(BW)
    for rec in range(2):
        rows = NB[rec].reshape(LEN, D)
        qkv = jnp.dot(rows, weight, preferred_element_type=jnp.float32)
        QKV[rec, HALO : LEN + HALO] = qkv.astype(jnp.bfloat16)
        if rec == 0:
            arrived(pxn)
            pyn = ring(near_y, at_y, RING_Y)
    arrived(pxf)
    pyf = ring(far_y, at_y, RING_Y)
    k2 = [same(BP.at[:, :, :, eighth], sibling)]
    oxn_start(2)
    arrived(of)
    oxf += ring(far_x, at_x, 0)
    k1 = [same(BO.at[:, x, :, part_b], sibling)]
    oaf = []
    if WA:
        arrived(oah)
        oaf = far(BO, slot_a)

    zeros = jnp.zeros((2, HALO, HDIM), jnp.bfloat16)
    QKV[:, 0:HALO, 0:HDIM] = zeros
    QKV[:, LEN + HALO : LEN + 2 * HALO, 0:HDIM] = zeros
    tall = 64 + 2 * HALO
    wide = 128 + 2 * HALO
    key_at = lax.broadcasted_iota(jnp.int32, (wide // 2, LEN), 1)

    def attention(k):
        chip = lax.rem(y + k, 4)
        for rec in range(2):
            keep = key_at < len_ref[rec]
            keys = QKV[rec, HALO : LEN + HALO, HDIM : 2 * HDIM]
            vals = QKV[rec, HALO : LEN + HALO, 2 * HDIM : 3 * HDIM]
            for part in range(2):
                first = pl.multiple_of(chip * 128 + part * (wide // 2), 16)
                query = QKV[rec, pl.ds(first, wide // 2), 0:HDIM]
                scores = lax.dot_general(
                    query, keys, (((1,), (1,)), ((), ())), preferred_element_type=jnp.float32
                )
                scores = jnp.where(keep, scores, -1e30)
                highest = jnp.max(scores, axis=-1, keepdims=True)
                powers = jnp.exp2((scores - highest) * (LOG2E * HDIM**-0.5))
                totals = jnp.sum(powers, axis=-1, keepdims=True)
                mixed = jnp.dot(
                    powers.astype(jnp.bfloat16), vals, preferred_element_type=jnp.float32
                )
                ATT[k, rec, part * (wide // 2) : (part + 1) * (wide // 2)] = (
                    mixed / totals
                ).astype(jnp.bfloat16)
        made = []
        for other in (0, 1):
            core = lax.rem(c + other, 2)
            rows = pl.ds(pl.multiple_of(core * 64, 64), tall)
            if k or other:
                device = {"seq": chip * 2 + core, "dp": d}
                made.append(copy(ATT.at[k, :, rows], A.at[:, :, eighth], device))
            else:
                A[:, :, eighth] = ATT[k, :, rows]
        return made

    a1 = attention(2) + attention(1)
    pyn2 = ring_on(near_y, at_y, pyn, RING_Y)
    k2 += [same(near_y(k, 2), sibling) for k in (1, 3)]
    a1 += attention(3) + attention(0)
    ring_on(near_x, at_x, oxn, 0)
    k1 += [same(near_x(k, 2), sibling) for k in (1, 3)]
    if WA:
        arrived(oan)
        k1 += [same(slot_a(BO, NEAR), sibling)]
    pyf2 = ring_on(far_y, at_y, pyf, RING_Y)
    k2 += [same(far_y(k, 2), sibling) for k in (1, 3)]
    arrived(oxn[2:])
    k1 += [same(near_x(2, 2), sibling)]
    ring_on(far_x, at_x, oxf, 0)
    k1 += [same(far_x(k, 2), sibling) for k in (1, 3)]
    arrived(oxf[2:])
    k1 += [same(far_x(2, 2), sibling)]
    if WA:
        arrived(oaf)
        k1 += [same(slot_a(BO, FAR), sibling)]
    arrived(h1)
    arrived(a1)
    arrived(k1)

    attended = A[...].reshape(2 * tall, D)
    projected = jnp.dot(attended, natural(BO), preferred_element_type=jnp.float32)
    resid = (FH[...].astype(jnp.float32) + projected.reshape(2, tall, D)).astype(jnp.bfloat16)
    FH[...] = resid
    position = s * 64 - HALO + lax.broadcasted_iota(jnp.int32, (tall, 1), 0)
    inside = (position >= 0) & (position < LEN)
    for rec in range(2):
        valid = inside & (position < len_ref[rec])
        normed = jnp.where(valid, norm_rows(resid[rec].astype(jnp.float32)), 0.0)
        CV[rec] = normed.astype(jnp.bfloat16).astype(jnp.float32)
    arrived(pyn2)
    k2 += [same(near_y(2, 2), sibling)]
    arrived(pyf2)
    k2 += [same(far_y(2, 2), sibling)]
    gated = []
    for rec in range(2):
        depth = jnp.zeros((64, D), jnp.float32)
        for tap in range(KERNEL):
            start = HALO - KERNEL // 2 + tap
            depth = depth + CV[rec, start : start + 64] * wd_ref[tap : tap + 1]
        gated.append((depth * jax.nn.sigmoid(depth)).astype(jnp.bfloat16))
    gated = jnp.concatenate(gated, axis=0)
    arrived(k2)
    pointed = jnp.dot(gated, natural(BP), preferred_element_type=jnp.float32)
    position = s * 64 + lax.broadcasted_iota(jnp.int32, (64, 1), 0)
    for rec in range(2):
        total = FH[rec, HALO : 64 + HALO].astype(jnp.float32) + pointed[rec * 64 : rec * 64 + 64]
        out_ref[rec] = jnp.where(position < len_ref[rec], total, 0.0).astype(jnp.bfloat16)
    for one in started:
        one.wait_send()


def body(frames, lengths, w_qkv, w_out, w_point, w_depth):
    vmem = pl.BlockSpec(memory_space=pltpu.VMEM)
    hbm = pl.BlockSpec(memory_space=pltpu.HBM)
    tall = 64 + 2 * HALO
    bf16 = jnp.bfloat16
    return pl.pallas_call(
        kernel,
        out_shape=jax.ShapeDtypeStruct((2, 64, D), bf16),
        in_specs=[hbm] * 6,
        out_specs=vmem,
        scratch_shapes=[
            pltpu.VMEM((2, 8, 64, D), bf16),
            pltpu.VMEM((2, tall, D), bf16),
            pltpu.VMEM((16, 4, 16, 3 * HDIM), bf16),
            pltpu.VMEM((16, 4, 16, D), bf16),
            pltpu.VMEM((16, 4, 16, D), bf16),
            pltpu.VMEM((2, LEN + 2 * HALO, 3 * HDIM), bf16),
            pltpu.VMEM((4, 2, 128 + 2 * HALO, HDIM), bf16),
            pltpu.VMEM((2, tall, D), bf16),
            pltpu.VMEM((2, tall, D), jnp.float32),
            pltpu.VMEM((KERNEL, D), jnp.float32),
            pltpu.SMEM((2,), jnp.int32),
            pltpu.SemaphoreType.DMA((N_SEM,)),
            pltpu.SemaphoreType.DMA((N_SEM,)),
            pltpu.SemaphoreType.DMA((8,)),
        ],
        compiler_params=pltpu.CompilerParams(
            collective_id=0, has_side_effects=True, vmem_limit_bytes=61 << 20
        ),
        name="conformer",
    )(lengths, frames, w_qkv, w_out, w_point, w_depth)


def solution(mesh):
    in_specs = (P("dp", "seq", None), P("dp"), P("dp", None), P("dp", None), P("dp", None), P())
    out_specs = P("dp", "seq", None)
    return jax.shard_map(body, mesh=mesh, in_specs=in_specs, out_specs=out_specs, check_vma=False)
```
